32 devices in a mesh: col: 8 (over z, core), tile: 4 (over y, x).
Axes of the slice: x: 2, y: 2, z: 4, core: 2. Of those that a mesh axis runs over, the one named last changes fastest.
Arguments:
- boundary: bfloat16 [8, 1024, 4, 1024], P('col', 'tile'), may hold values from -6 to 6
- row_tensors: bfloat16 [8, 4, 4, 4, 4], P('col'), may hold values from -3 to 3
- sketch_bond: bfloat16 [8, 1024, 1024], P('col', 'tile'), may hold values from -0.1875 to 0.1875
- sketch_phys: bfloat16 [8, 4, 4, 1024], P('col'), may hold values from -6 to 6
- edge_factor: bfloat16 [1024, 4, 1024], P('tile'), may hold values from -0.09375 to 0.09375
- closing: float32 [8, 4], P('col'), may hold values from 0.2 to 2
- left_edge: float32 [1024], replicated, may hold values from -6 to 6
Outputs:
- new_boundary: bfloat16 [8, 1024, 4, 1024], P('col', 'tile')
- envs: float32 [8, 1024], P('col', 'tile')
The draws below stay inside these ranges and needn't reach their ends.
All inputs are finite; a program needn't handle non-finite values.
Results may differ from the reference program's by a relative error of at most 0.012.
The reference program's roundings to bfloat16 on the way count: a program that leaves them out, or rounds other values in their place, can miss the bound.
Values may be sent and summed in bfloat16 or wider, within the bound.
No kernel may reach another device: no remote copies, remote signals or barrier semaphores. Data moves between devices by JAX's collectives and lax.ppermute only.
A program may use at most 128 MiB of HBM per device.

```python
import math
import jax
import jax.numpy as jnp
from jax import lax

CHI = 1024
D = 4
COLS = 8


def block_levels(rng, extent, cuts, smallest, top_value):
    factor_of = 1.0
    for dim, shards_of in cuts:
        heights = jax.random.uniform(jax.random.fold_in(jax.random.fold_in(rng, 6), dim), (shards_of,), jnp.float32, smallest / len(cuts), top_value / len(cuts))
        factor_of = factor_of * jnp.repeat(jnp.exp(heights), extent[dim] // shards_of).reshape((-1,) + (1,) * (len(extent) - 1 - dim))
    return factor_of


def normal_values(rng, dims, spread, limit, split=(), held_as=jnp.bfloat16):
    array = spread * jax.random.normal(rng, dims, jnp.float32)
    if split:
        array = array * block_levels(rng, dims, split, -0.22, 0.18)
    return jnp.clip(array, -limit, limit).astype(held_as)


def setup_inputs(seed: int = 0) -> dict:
    streams_of = jax.random.split(jax.random.key(seed), 8)
    boundary = normal_values(streams_of[0], (COLS, CHI, D, CHI), 1.0, 6.0, ((0, 8), (1, 4)))
    row_tensors = normal_values(streams_of[1], (COLS, D, D, D, D), 0.5, 3.0, ((0, 8),))
    sketch_bond = normal_values(streams_of[2], (COLS, CHI, CHI), CHI ** -0.5, 0.1875, ((0, 8), (1, 4)))
    sketch_phys = normal_values(streams_of[3], (COLS, D, D, CHI), 1.0, 6.0, ((0, 8),))
    edge_factor = normal_values(streams_of[4], (CHI, D, CHI), (CHI * D) ** -0.5, 0.09375, ((0, 4),))
    closing = jnp.clip(jnp.exp(math.log(2.0) - 2.3025851 * jax.random.uniform(streams_of[5], (COLS, D), jnp.float32) ** block_levels(streams_of[5], (COLS, D), ((0, 8),), -0.2, 0.2)), 0.2, 2.0)
    left_edge = normal_values(streams_of[6], (CHI,), 1.0, 6.0, (), jnp.float32)
    return {"boundary": boundary, "row_tensors": row_tensors, "sketch_bond": sketch_bond, "sketch_phys": sketch_phys, "edge_factor": edge_factor, "closing": closing, "left_edge": left_edge}


GRAM_SHIFT = 0.001

def reference(boundary, row_tensors, sketch_bond, sketch_phys, edge_factor, closing, left_edge):
    highest = lax.Precision.HIGHEST
    left_basis = edge_factor
    sites = []
    for column in range(COLS):
        own_site = boundary[column].astype(jnp.float32)
        row_tensor = row_tensors[column].astype(jnp.float32)
        phys_map = jnp.einsum('lurd,ldk->urk', row_tensor, sketch_phys[column].astype(jnp.float32), precision=highest)
        sketched = jnp.einsum('bua,ka->buk', own_site, sketch_bond[column].astype(jnp.float32), precision=highest)
        range_rows = lax.optimization_barrier(jnp.sum(sketched[:, :, None, :] * phys_map[None], axis=1))
        range_flat = range_rows.reshape(CHI * D, CHI)
        gram = jnp.dot(range_flat.T, range_flat, precision=highest) + GRAM_SHIFT * jnp.eye(CHI, dtype=jnp.float32)
        lower_factor = jnp.linalg.cholesky(gram)
        basis = jax.scipy.linalg.solve_triangular(lower_factor, range_flat.T, lower=True).T
        basis = basis.astype(jnp.bfloat16).reshape(CHI, D, CHI)
        right_part = jnp.einsum('bua,brk->aurk', own_site, basis.astype(jnp.float32), precision=highest)
        absorbed = jnp.einsum('aurk,lurd->aldk', right_part, row_tensor, precision=highest)
        new_site = jnp.einsum('alc,aldk->kdc', left_basis.astype(jnp.float32), absorbed, precision=highest)
        sites.append(new_site.astype(jnp.bfloat16))
        left_basis = basis
    new_boundary = jnp.stack(sites)
    environment = left_edge
    envs = []
    for column in range(COLS):
        transfer = jnp.einsum('kdc,d->kc', new_boundary[column].astype(jnp.float32), closing[column], precision=highest).astype(jnp.bfloat16)
        weighted = jnp.dot(transfer.astype(jnp.float32), environment, precision=highest)
        environment = weighted * jnp.sqrt(jnp.float32(CHI)) / jnp.sqrt(jnp.sum(weighted * weighted) + 1e-06)
        envs.append(environment)
    return (new_boundary, jnp.stack(envs))
```

```python
import functools

import jax
import jax.numpy as jnp
from jax import lax
from jax.experimental import pallas as pl
from jax.experimental.pallas import tpu as pltpu
from jax.sharding import PartitionSpec as P

GRAM_SHIFT = 0.001
F32 = jnp.float32
BF16 = jnp.bfloat16
LANES = 128
SUB = 8
VMEM = pltpu.VMEM
NT = ((1,), (1,))
NN = ((1,), (0,))
AXES = ("col", "tile")


def passed_along(block, axis, distance):
    devices = range(lax.axis_size(axis))
    route = [(i - distance, i) for i in devices if i - distance in devices]
    return lax.ppermute(block, axis, route)


def plain(boundary, row_tensors, sketch_bond, sketch_phys, edge_factor, closing, left_edge):
    highest = lax.Precision.HIGHEST
    own_site = boundary[0]
    row_tensor = row_tensors[0].astype(jnp.float32)
    bond_sketch = sketch_bond[0]
    phys_map = jnp.einsum(
        "lurd,ldk->urk", row_tensor, sketch_phys[0].astype(jnp.float32), precision=highest
    )
    local_rows = own_site.shape[0]
    legs = own_site.shape[1]
    width = own_site.shape[2]
    sketched = jnp.einsum(
        "bua,ka->buk",
        own_site,
        lax.all_gather(bond_sketch, "tile", axis=0, tiled=True),
        preferred_element_type=jnp.float32,
    )
    range_rows = jnp.sum(sketched[:, :, None, :] * phys_map[None], axis=1)
    range_flat = range_rows.reshape(local_rows * legs, width)
    gram_local = jnp.dot(range_flat.T, range_flat, precision=highest)
    gram_total = lax.psum(gram_local, "tile") + GRAM_SHIFT * jnp.eye(width, dtype=jnp.float32)
    lower_factor = jnp.linalg.cholesky(gram_total)
    basis = jax.scipy.linalg.solve_triangular(lower_factor, range_flat.T, lower=True).T
    basis = basis.astype(jnp.bfloat16).reshape(local_rows, legs, width)
    arrived = passed_along(basis, "col", 1)
    first_column = lax.axis_index("col") == 0
    left_basis = jnp.where(first_column, edge_factor, arrived)
    basis_cols = lax.all_to_all(basis, "tile", split_axis=2, concat_axis=0, tiled=True)
    matching = basis_cols
    right_part = jnp.einsum(
        "bua,brk->aurk",
        lax.all_gather(own_site, "tile", axis=0, tiled=True),
        matching,
        preferred_element_type=jnp.float32,
    )
    absorbed = jnp.einsum("aurk,lurd->aldk", right_part, row_tensor, precision=highest)
    matching = absorbed
    new_site = jnp.einsum(
        "alc,aldk->kdc",
        lax.all_gather(left_basis, "tile", axis=0, tiled=True).astype(jnp.float32),
        matching,
        precision=highest,
    )
    new_site = new_site.astype(jnp.bfloat16)
    transfer_rows = jnp.einsum(
        "kdc,d->kc", new_site.astype(jnp.float32), closing[0], precision=highest
    ).astype(jnp.bfloat16)
    scale = jnp.sqrt(jnp.float32(width))
    column_count = lax.axis_size("col")
    share = transfer_rows.shape[0]
    transfer_local = transfer_rows.astype(jnp.float32)

    def relay_split(turn_index, current):
        incoming = passed_along(current, "col", 1)
        incoming_whole = lax.all_gather(incoming, "tile", axis=0, tiled=True)
        incoming_whole = jnp.where(first_column, left_edge, incoming_whole)
        weighted = jnp.dot(transfer_local, incoming_whole, precision=highest)
        squares = lax.psum(jnp.sum(weighted * weighted), "tile")
        return weighted * scale / jnp.sqrt(squares + 1e-06)

    env_local = lax.fori_loop(0, column_count, relay_split, jnp.zeros((share,), jnp.float32))
    return (new_site[None], env_local[None])


def call(kernel, name, flops, vmem, **kwargs):
    return pl.pallas_call(
        kernel,
        name=name,
        compiler_params=pltpu.CompilerParams(vmem_limit_bytes=vmem * 2**20),
        cost_estimate=pl.CostEstimate(flops=int(flops), bytes_accessed=1 << 20, transcendentals=0),
        **kwargs,
    )


def whole(count):
    return [pl.BlockSpec(memory_space=VMEM)] * count


def scalars(count):
    return [pl.BlockSpec(memory_space=pltpu.SMEM)] * count


def two_parts(x):
    hi = x.astype(BF16)
    return hi, (x - hi.astype(F32)).astype(BF16)


def dot1(a, b, dims):
    return lax.dot_general(a, b, (dims, ((), ())), preferred_element_type=F32)


def dot3(a, b, dims):
    (ah, al), (bh, bl) = a, b
    return dot1(ah, bh, dims) + (dot1(ah, bl, dims) + dot1(al, bh, dims))


def spread(x):
    return jnp.broadcast_to(x, (SUB, LANES))


def factor_panel(s):
    s = dict(s)
    inv = {}
    for c in range(SUB):
        rs = lax.rsqrt(s[c, c])
        low = {r: s[r, c] * rs for r in range(c + 1, SUB)}
        for r in range(c + 1, SUB):
            for q in range(c + 1, r + 1):
                s[r, q] = s[r, q] - low[r] * low[q]
        for q in range(c):
            inv[c, q] = inv[c, q] * rs
        inv[c, c] = rs
        for r in range(c + 1, SUB):
            for q in range(c + 1):
                term = low[r] * inv[c, q]
                inv[r, q] = inv[r, q] - term if (r, q) in inv else -term
    return inv


def inverse_factor(block):
    n = LANES // SUB
    row = lax.broadcasted_iota(jnp.int32, (SUB, LANES), 0)
    lane = lax.broadcasted_iota(jnp.int32, (SUB, LANES), 1)
    zero = jnp.zeros((SUB, LANES), F32)
    a = [block[SUB * i : SUB * (i + 1), :] for i in range(n)]
    e = [jnp.where(lane == row + SUB * i, 1.0, 0.0).astype(F32) for i in range(n)]
    out = []
    for p in range(n):
        u, eu = a[p], e[p]
        cols = [spread(u[:, SUB * p + c : SUB * p + c + 1]) for c in range(SUB)]
        inv = factor_panel({(r, c): spread(cols[c][r : r + 1, :]) for c in range(SUB) for r in range(c, SUB)})
        w, we = zero, zero
        for c in range(SUB):
            m = zero
            for r in range(c, SUB):
                m = jnp.where(row == r, inv[r, c], m)
            if p < n - 1:
                w = w + m * spread(u[c : c + 1, :])
            we = we + m * spread(eu[c : c + 1, :])
        out.append(we)
        if p == n - 1:
            break
        v, ve = zero, zero
        for q in range(SUB):
            m = zero
            for c in range(q + 1):
                m = jnp.where(row == c, inv[q, c], m)
            v = v + m * spread(w[q : q + 1, :])
            ve = ve + m * spread(we[q : q + 1, :])
        vs = [spread(v[c : c + 1, :]) for c in range(SUB)]
        ves = [spread(ve[c : c + 1, :]) for c in range(SUB)]
        for i in range(p + 1, n):
            for c in range(SUB):
                low = spread(a[i][:, SUB * p + c : SUB * p + c + 1]) if c == 0 else lows[c]
                if c == 0:
                    lows = [low] + [spread(a[i][:, SUB * p + k : SUB * p + k + 1]) for k in range(1, SUB)]
                a[i] = a[i] - low * vs[c]
                e[i] = e[i] - low * ves[c]
    return jnp.concatenate(out, 0)


def sketch_kernel(parts, first, where_ref, map_ref, *refs):
    bonds, site, refs = refs[:parts], refs[parts], refs[parts + 1 :]
    legs, share, _ = site.shape
    size = bonds[0].shape[0]
    before = () if first else refs[:parts]
    rows_ref, panels, high, low = refs[0 if first else parts], refs[-2 - parts : -2], refs[-2], refs[-1]
    for n in range(parts):
        at = pl.ds(pl.multiple_of(where_ref[n] * size, size), size)
        sk = [dot1(bonds[n][...], site[u], NT) for u in range(legs)]
        for r in range(legs):
            total = sk[0] * map_ref[at, r : r + 1]
            for u in range(1, legs):
                total = total + sk[u] * map_ref[at, u * legs + r : u * legs + r + 1]
            rows_ref[at, r * share : (r + 1) * share] = total
            hi, lo = two_parts(total)
            high[at, r * share : (r + 1) * share] = hi
            low[at, r * share : (r + 1) * share] = lo
    for j in range(parts):
        right = (high[j * size : (j + 1) * size, :], low[j * size : (j + 1) * size, :])
        for i in range(j, parts):
            left = (high[i * size : (i + 1) * size, :], low[i * size : (i + 1) * size, :])
            block = dot3(left, right, NT)
            at = slice((i - j) * size, (i - j + 1) * size)
            if not first:
                block = block + before[j][at, :]
            panels[j][at, :] = block


def sketch(where, phys, bonds, site, before):
    parts = len(bonds)
    size, width = bonds[0].shape
    legs, share, _ = site.shape
    shapes = [jax.ShapeDtypeStruct((width, legs * share), F32)]
    shapes += [jax.ShapeDtypeStruct((width - j * size, size), F32) for j in range(parts)]
    out = call(
        functools.partial(sketch_kernel, parts, not before),
        "sketch",
        5e9,
        48,
        out_shape=shapes,
        in_specs=scalars(1) + whole(parts + 2 + len(before)),
        out_specs=whole(parts + 1),
        scratch_shapes=[VMEM((width, legs * share), BF16)] * 2,
    )(where, phys, *bonds, site, *before)
    return out[0], list(out[1:])


def basis_kernel(turn, groups, last, *refs):
    own, other, refs = refs[0], refs[1], refs[2:]
    lows, refs = refs[:turn], refs[turn:]
    highs, refs = refs[:turn], refs[turn:]
    rests, refs = refs[:turn], refs[turn:]
    rows, refs = refs[:groups], refs[groups:]
    size = own.shape[1]
    half = size // 2
    s = own[...] + other[...]
    row = lax.broadcasted_iota(jnp.int32, s.shape, 0)
    lane = lax.broadcasted_iota(jnp.int32, s.shape, 1)
    s = s + jnp.where(row == lane, GRAM_SHIFT, 0.0).astype(F32)
    facing = []
    for i in range(turn):
        at = (turn - i - 1) * size
        below = two_parts(lows[i][at:, :])
        facing.append((below[0][:size], below[1][:size]))
        s = s - dot3(below, facing[i], NT)
    x1 = inverse_factor(s[:half, :half])
    x1p = two_parts(x1)
    l21p = two_parts(dot3(two_parts(s[half:size, :half]), x1p, NT))
    x2 = inverse_factor(s[half:size, half:] - dot3(l21p, l21p, NT))
    x2p = two_parts(x2)
    x21 = -dot3(x2p, two_parts(dot3(l21p, x1p, NN)), NN)
    inv = jnp.concatenate(
        [jnp.concatenate([x1, jnp.zeros((half, half), F32)], 1), jnp.concatenate([x21, x2], 1)], 0
    )
    inv = two_parts(inv)
    if not last:
        refs[0][...] = dot3(two_parts(s[size:, :]), inv, NT)
    for g in range(groups):
        part = rows[g][...]
        for i in range(turn):
            part = part - dot3(facing[i], (highs[i][g], rests[i][g]), NN)
        hi, lo = two_parts(dot3(inv, two_parts(part), NN))
        if last:
            refs[0][g] = hi
        else:
            refs[1][g] = hi
            refs[2][g] = lo


def basis_columns(turn, own, other, lows, highs, rests, rows):
    size = own.shape[1]
    groups = len(rows)
    last = own.shape[0] == size
    cols = jax.ShapeDtypeStruct((groups, size, rows[0].shape[1]), BF16)
    shapes = [cols] if last else [jax.ShapeDtypeStruct((own.shape[0] - size, size), F32), cols, cols]
    rows_spec = pl.BlockSpec((size, rows[0].shape[1]), lambda i: (turn, 0))
    return call(
        functools.partial(basis_kernel, turn, groups, last),
        "basis",
        15e9,
        56,
        out_shape=shapes,
        grid=(1,),
        in_specs=whole(2 + 3 * turn) + [rows_spec] * groups,
        out_specs=whole(len(shapes)),
    )(own, other, *lows, *highs, *rests, *rows)


def absorb_kernel(legs, mix_ref, basis_a, basis_b, site_a, site_b, out_ref, held):
    groups, size, wide = basis_a.shape
    share = wide // legs
    step = mix_ref.shape[0] // (legs * legs)
    for u in range(legs):
        for r in range(legs):
            at = slice(r * share, (r + 1) * share)
            total = None
            for basis, site in ((basis_a, site_a), (basis_b, site_b)):
                for g in range(groups):
                    term = dot1(basis[g, :, at], site[g, u], NN)
                    total = term if total is None else total + term
            held[u * legs + r] = total.astype(BF16)
    block = held.shape[2]
    for n in range(size // step):
        rows = slice(n * step, (n + 1) * step)
        stack = jnp.concatenate([held[m, rows, :] for m in range(legs * legs)], 0)
        mixed = dot1(mix_ref[...], stack, NN).astype(BF16)
        for d in range(legs):
            for l in range(legs):
                m = (d * legs + l) * step
                out_ref[0, d * size + n * step : d * size + (n + 1) * step, l * block : (l + 1) * block] = mixed[
                    m : m + step
                ]


def absorb(mix, basis_a, basis_b, site_a, site_b):
    groups, size, wide = basis_a.shape
    _, legs, share, width = site_a.shape
    parts = width // size
    site_spec = pl.BlockSpec((groups, legs, share, size), lambda i: (0, 0, 0, i))
    return call(
        functools.partial(absorb_kernel, legs),
        "absorb",
        15e9,
        48,
        out_shape=jax.ShapeDtypeStruct((parts, legs * size, legs * size), BF16),
        grid=(parts,),
        in_specs=whole(3) + [site_spec] * 2,
        out_specs=pl.BlockSpec((1, legs * size, legs * size), lambda i: (i, 0, 0)),
        scratch_shapes=[VMEM((legs * legs, size, size), BF16)],
    )(mix, basis_a, basis_b, site_a, site_b)


def close_kernel(parts, legs, where_ref, weights, absorbed, *refs):
    lefts, site_ref, transfer_ref, total = refs[:parts], refs[parts], refs[parts + 1], refs[parts + 2]
    n = pl.program_id(0)

    @pl.when(n == 0)
    def _():
        total[...] = jnp.zeros_like(total)

    for i in range(parts):

        @pl.when(n == i)
        def _():
            total[...] += dot1(absorbed[0], lefts[i][...], NT)

    @pl.when(n == parts - 1)
    def _():
        size = transfer_ref.shape[0]
        closed = None
        for d in range(legs):
            part = total[d * size : (d + 1) * size, :].astype(BF16)
            site_ref[d] = part
            term = part.astype(F32) * weights[d]
            closed = term if closed is None else closed + term
        transfer_ref[...] = closed.astype(BF16)


def close(where, weights, absorbed, lefts):
    parts, tall, wide = absorbed.shape
    legs = weights.shape[0]
    size, block = tall // legs, lefts[0].shape[0]
    return call(
        functools.partial(close_kernel, parts, legs),
        "close",
        3e9,
        48,
        out_shape=[
            jax.ShapeDtypeStruct((legs, size, block), BF16),
            jax.ShapeDtypeStruct((size, block), BF16),
        ],
        grid_spec=pltpu.PrefetchScalarGridSpec(
            num_scalar_prefetch=1,
            grid=(parts,),
            in_specs=scalars(1)
            + [pl.BlockSpec((1, tall, wide), lambda i, where: (where[i], 0, 0))]
            + whole(parts),
            out_specs=whole(2),
            scratch_shapes=[VMEM((tall, block), F32)],
        ),
    )(where, weights, absorbed, *lefts)


def relay_kernel(parts, info, coming, kept, *refs):
    transfers, out, weighted = refs[:parts], refs[parts], refs[parts + 1]
    size, width = transfers[0].shape
    whole_env = coming[...]
    first = whole_env.astype(BF16)
    left = whole_env - first.astype(F32)
    second = left.astype(BF16)
    third = (left - second.astype(F32)).astype(BF16)
    row = lax.broadcasted_iota(jnp.int32, (16, width), 0)
    grow = lambda v: jnp.broadcast_to(v.astype(F32), (16, width))
    lhs = jnp.where(row == 0, grow(first), jnp.where(row == 1, grow(second), jnp.where(row == 2, grow(third), 0.0)))
    lhs = lhs.astype(BF16)
    for n in range(parts):
        product = dot1(lhs, transfers[n][...], NT)
        at = pl.ds(pl.multiple_of(info[n] * size, size), size)
        weighted[:, at] = jnp.sum(product, axis=0, keepdims=True)
    w = weighted[...]
    squares = jnp.sum(w * w, axis=1, keepdims=True)
    env = w * jnp.sqrt(jnp.float32(width)) / jnp.sqrt(squares + 1e-06)
    out[...] = jnp.where(info[parts] == 1, env, kept[...])


def relay(info, coming, kept, transfers):
    parts = len(transfers)
    return call(
        functools.partial(relay_kernel, parts),
        "relay",
        1e8,
        24,
        out_shape=jax.ShapeDtypeStruct(kept.shape, F32),
        in_specs=scalars(1) + whole(2 + parts),
        out_specs=pl.BlockSpec(memory_space=VMEM),
        scratch_shapes=[VMEM(kept.shape, F32)],
    )(info, coming, kept, *transfers)


def paired(columns, tiles, boundary, row_tensors, sketch_bond, sketch_phys, edge_factor, closing, left_edge):
    planes, rows = columns // 2, tiles // 2

    def number(z, c, y, x):
        return (2 * z + c) * tiles + 2 * y + x

    every = [(z, c, y, x) for z in range(planes) for c in range(2) for y in range(rows) for x in range(2)]

    def which(z, x):
        return x ^ (z & 1)

    def fetch(i):
        return [(number(z, which(z, x), (y + i) % rows, x ^ c), number(z, c, y, x)) for z, c, y, x in every]

    home = [(b, a) for a, b in fetch(0)]
    core = [(number(z, c, y, x), number(z, 1 - c, y, x)) for z, c, y, x in every]
    cross = [(number(z, c, y, x), number(z, c, y, 1 - x)) for z, c, y, x in every]

    def turned(i):
        return [(number(z, c, (y + i) % rows, x), number(z, c, y, x)) for z, c, y, x in every]

    def right_of(z, c, y, x):
        if which(z, x) == 0:
            return number(z, c, y, 1 - x)
        return number(z + 1, c, y, x) if z + 1 < planes else None

    right = [(number(*d), right_of(*d)) for d in every if right_of(*d) is not None]
    edge_route = [(number(0, 1, y, 1), number(0, 1, y, 0)) for y in range(rows)]

    def move(block, route):
        return lax.ppermute(block, AXES, route)

    col, tile = lax.axis_index("col"), lax.axis_index("tile")
    z, c, y, x = col // 2, col % 2, tile // 2, tile % 2
    s = (x + z) % 2
    site_number = 2 * z + s
    own_column = c == s

    share, legs, width = boundary.shape[1:]
    size = width // tiles

    small = jnp.concatenate(
        [
            sketch_phys[0].reshape(legs * legs, width).astype(F32),
            jnp.pad(
                jnp.concatenate([row_tensors[0].reshape(-1).astype(F32), closing[0]]),
                (0, width - legs**4 - legs),
            )[None],
        ]
    )
    small = jnp.where(own_column, small, move(small, core))
    row_tensor = small[-1, : legs**4].reshape(legs, legs, legs, legs)
    weights = small[-1, legs**4 : legs**4 + legs]
    phys_map = jnp.einsum(
        "lurd,ldk->kur",
        row_tensor,
        small[:-1].reshape(legs, legs, width),
        precision=lax.Precision.HIGHEST,
    ).reshape(width, legs * legs)
    step = size // (legs * legs)
    mix = jnp.einsum("lurd,ab->dlaurb", row_tensor, jnp.eye(step, dtype=F32))
    mix = mix.reshape(legs * legs * step, legs * legs * step).astype(BF16)

    ahead = jnp.arange(rows, dtype=jnp.int32)
    near = 2 * ((y + ahead) % rows) + (x + c) % 2
    far = 2 * ((y + ahead) % rows) + (x + c + 1) % 2
    spots = jnp.concatenate([near, far]).astype(jnp.int32)

    bonds = [move(sketch_bond[0], fetch(i)) for i in range(rows)]
    bonds += [move(b, core) for b in bonds]
    site = boundary[0].transpose(1, 0, 2)
    sites = [move(site, fetch(i)) for i in range(rows)]

    range_rows, panels = [], []
    for block in sites:
        rows_t, panels = sketch(spots, phys_map, bonds, block, panels)
        range_rows.append(rows_t)
    others = [move(p, core) for p in panels]
    site_a = jnp.stack(sites)
    site_a, _ = lax.optimization_barrier((site_a, others[0]))
    site_b = move(site_a, core)

    edge, _ = lax.optimization_barrier((edge_factor, others[0]))
    edge = jnp.where(c == 0, edge, move(edge, edge_route))
    edge = edge.transpose(2, 1, 0).reshape(width, legs * share)

    lows, highs, rests, lefts = [], [], [], []
    for turn in range(tiles):
        out = basis_columns(turn, panels[turn], others[turn], lows, highs, rests, range_rows)
        if turn < tiles - 1:
            lows.append(out[0])
            rests.append(out[2])
        highs.append(out[-1] if turn == tiles - 1 else out[1])
        come = move(highs[turn][0], right)
        come = jnp.where(site_number == 0, edge[turn * size : (turn + 1) * size], come)
        mine = [come] + [move(come, turned(i)) for i in range(1, rows)]
        lefts.append(mine + [move(m, core) for m in mine])

    def picked(q):
        out = highs[0]
        for turn in range(1, tiles):
            out = jnp.where(q == turn, highs[turn], out)
        return out

    basis_b = move(picked(far[0]), core)
    absorbed = absorb(mix, picked(near[0]), basis_b, site_a, site_b)

    source = jnp.where(s == 1, 1 - x, x)
    near_left = 2 * ((y + ahead) % rows) + (source + c) % 2
    far_left = 2 * ((y + ahead) % rows) + (source + c + 1) % 2
    left_spots = jnp.concatenate([near_left, far_left]).astype(jnp.int32)
    new_parts, transfer_parts = [], []
    for turn in range(tiles):
        new, transfer = close(left_spots, weights, absorbed, lefts[turn])
        new_parts.append(move(new, home))
        transfer_parts.append(transfer)
    new_site = jnp.concatenate(new_parts, axis=2).transpose(1, 0, 2)

    transfer = jnp.concatenate(transfer_parts, axis=1)
    transfers = [transfer] + [move(transfer, turned(i)) for i in range(1, rows)]
    transfers += [move(t, core) for t in transfers]

    env = left_edge[None]
    kept = env
    for turn in range(columns):
        if turn:
            route = [(a, b) for (a, b), d in zip(right, (d for d in every if right_of(*d) is not None)) if 2 * d[0] + which(d[0], d[3]) == turn - 1]
            env = move(kept, route)
        info = jnp.concatenate([spots, (site_number == turn).astype(jnp.int32)[None]])
        kept = relay(info, env, kept, transfers)
    env = jnp.where(own_column, kept, move(kept, cross))
    env = lax.dynamic_slice_in_dim(env, tile * share, share, axis=1)
    return new_site[None], env


def solution(mesh):
    in_specs = (
        P("col", "tile", None, None),
        P("col", None, None, None, None),
        P("col", "tile", None),
        P("col", None, None, None),
        P("tile", None, None),
        P("col", None),
        P(),
    )
    out_specs = (P("col", "tile", None, None), P("col", "tile"))
    columns, tiles = mesh.shape["col"], mesh.shape["tile"]

    def local(*args):
        share, legs, width = args[0].shape[1:]
        even = columns % 2 == 0 and tiles % 2 == 0
        if even and share % (2 * LANES) == 0 and share == width // tiles and legs**4 + legs <= width:
            return paired(columns, tiles, *args)
        return plain(*args)

    return jax.shard_map(local, mesh=mesh, in_specs=in_specs, out_specs=out_specs, check_vma=False)
```

```python
import functools

import jax
import jax.numpy as jnp
from jax import lax
from jax.experimental import pallas as pl
from jax.experimental.pallas import tpu as pltpu
from jax.sharding import PartitionSpec as P

GRAM_SHIFT = 0.001
F32 = jnp.float32
BF16 = jnp.bfloat16
LANES = 128
SUB = 8
VMEM = pltpu.VMEM
NT = ((1,), (1,))
NN = ((1,), (0,))
AXES = ("col", "tile")


def passed_along(block, axis, distance):
    devices = range(lax.axis_size(axis))
    route = [(i - distance, i) for i in devices if i - distance in devices]
    return lax.ppermute(block, axis, route)


def plain(boundary, row_tensors, sketch_bond, sketch_phys, edge_factor, closing, left_edge):
    highest = lax.Precision.HIGHEST
    own_site = boundary[0]
    row_tensor = row_tensors[0].astype(jnp.float32)
    bond_sketch = sketch_bond[0]
    phys_map = jnp.einsum(
        "lurd,ldk->urk", row_tensor, sketch_phys[0].astype(jnp.float32), precision=highest
    )
    local_rows = own_site.shape[0]
    legs = own_site.shape[1]
    width = own_site.shape[2]
    sketched = jnp.einsum(
        "bua,ka->buk",
        own_site,
        lax.all_gather(bond_sketch, "tile", axis=0, tiled=True),
        preferred_element_type=jnp.float32,
    )
    range_rows = jnp.sum(sketched[:, :, None, :] * phys_map[None], axis=1)
    range_flat = range_rows.reshape(local_rows * legs, width)
    gram_local = jnp.dot(range_flat.T, range_flat, precision=highest)
    gram_total = lax.psum(gram_local, "tile") + GRAM_SHIFT * jnp.eye(width, dtype=jnp.float32)
    lower_factor = jnp.linalg.cholesky(gram_total)
    basis = jax.scipy.linalg.solve_triangular(lower_factor, range_flat.T, lower=True).T
    basis = basis.astype(jnp.bfloat16).reshape(local_rows, legs, width)
    arrived = passed_along(basis, "col", 1)
    first_column = lax.axis_index("col") == 0
    left_basis = jnp.where(first_column, edge_factor, arrived)
    basis_cols = lax.all_to_all(basis, "tile", split_axis=2, concat_axis=0, tiled=True)
    matching = basis_cols
    right_part = jnp.einsum(
        "bua,brk->aurk",
        lax.all_gather(own_site, "tile", axis=0, tiled=True),
        matching,
        preferred_element_type=jnp.float32,
    )
    absorbed = jnp.einsum("aurk,lurd->aldk", right_part, row_tensor, precision=highest)
    matching = absorbed
    new_site = jnp.einsum(
        "alc,aldk->kdc",
        lax.all_gather(left_basis, "tile", axis=0, tiled=True).astype(jnp.float32),
        matching,
        precision=highest,
    )
    new_site = new_site.astype(jnp.bfloat16)
    transfer_rows = jnp.einsum(
        "kdc,d->kc", new_site.astype(jnp.float32), closing[0], precision=highest
    ).astype(jnp.bfloat16)
    scale = jnp.sqrt(jnp.float32(width))
    column_count = lax.axis_size("col")
    share = transfer_rows.shape[0]
    transfer_local = transfer_rows.astype(jnp.float32)

    def relay_split(turn_index, current):
        incoming = passed_along(current, "col", 1)
        incoming_whole = lax.all_gather(incoming, "tile", axis=0, tiled=True)
        incoming_whole = jnp.where(first_column, left_edge, incoming_whole)
        weighted = jnp.dot(transfer_local, incoming_whole, precision=highest)
        squares = lax.psum(jnp.sum(weighted * weighted), "tile")
        return weighted * scale / jnp.sqrt(squares + 1e-06)

    env_local = lax.fori_loop(0, column_count, relay_split, jnp.zeros((share,), jnp.float32))
    return (new_site[None], env_local[None])


def call(kernel, name, flops, vmem, **kwargs):
    return pl.pallas_call(
        kernel,
        name=name,
        compiler_params=pltpu.CompilerParams(vmem_limit_bytes=vmem * 2**20),
        cost_estimate=pl.CostEstimate(flops=int(flops), bytes_accessed=1 << 20, transcendentals=0),
        **kwargs,
    )


def whole(count):
    return [pl.BlockSpec(memory_space=VMEM)] * count


def anywhere(count):
    return [pl.BlockSpec(memory_space=pl.ANY)] * count


def scalars(count):
    return [pl.BlockSpec(memory_space=pltpu.SMEM)] * count


def two_parts(x):
    hi = x.astype(BF16)
    return hi, (x - hi.astype(F32)).astype(BF16)


def dot1(a, b, dims):
    return lax.dot_general(a, b, (dims, ((), ())), preferred_element_type=F32)


def dot3(a, b, dims):
    (ah, al), (bh, bl) = a, b
    return dot1(ah, bh, dims) + (dot1(ah, bl, dims) + dot1(al, bh, dims))


def spread(x):
    return jnp.broadcast_to(x, (SUB, LANES))


def summed(terms):
    terms = list(terms)
    while len(terms) > 1:
        terms = [terms[i] + terms[i + 1] if i + 1 < len(terms) else terms[i] for i in range(0, len(terms), 2)]
    return terms[0]


def chosen(bits, entries):
    entries = list(entries)
    for bit in bits:
        entries = [
            entries[i] if entries[i] is entries[i + 1] else jnp.where(bit, entries[i + 1], entries[i])
            for i in range(0, len(entries), 2)
        ]
    return entries[0]


def factor_panel(s):
    s = dict(s)
    inv = {}
    full = {}
    for c in range(SUB):
        rs = lax.rsqrt(s[c, c])
        low = {r: s[r, c] * rs for r in range(c + 1, SUB)}
        for r in range(c + 1, SUB):
            for q in range(c + 1, r + 1):
                s[r, q] = s[r, q] - low[r] * low[q]
        for q in range(c):
            inv[c, q] = inv[c, q] * rs
        inv[c, c] = rs
        for r in range(c + 1, SUB):
            for q in range(c + 1):
                term = low[r] * inv[c, q]
                inv[r, q] = inv[r, q] - term if (r, q) in inv else -term
        for r in range(c + 1):
            for q in range(r + 1):
                term = inv[c, r] * inv[c, q]
                full[r, q] = full[r, q] + term if (r, q) in full else term
    return inv, full


def inverse_factor(block, scratch):
    n = LANES // SUB
    row = lax.broadcasted_iota(jnp.int32, (SUB, LANES), 0)
    lane = lax.broadcasted_iota(jnp.int32, (SUB, LANES), 1)
    bits = [(row & b) != 0 for b in (1, 2, 4)]
    zero = jnp.zeros((SUB, LANES), F32)
    a = [block[SUB * i : SUB * (i + 1), :] for i in range(n)]
    e = [jnp.where(lane == row + SUB * i, 1.0, 0.0).astype(F32) for i in range(n)]
    used = 0

    def rows_of(registers):
        nonlocal used
        base, used = used, used + len(registers)
        for k, register in enumerate(registers):
            scratch[(base + k) * SUB : (base + k + 1) * SUB, :] = register
        return lambda k, r: scratch[pl.ds((base + k) * SUB + r, SUB, stride=0), :]

    out = []
    for p in range(n):
        u, eu = a[p], e[p]
        get = rows_of([spread(u[:, SUB * p + c : SUB * p + c + 1]) for c in range(SUB)] + [u, eu])
        inv, full = factor_panel({(r, c): get(c, r) for c in range(SUB) for r in range(c, SUB)})
        eus = [get(SUB + 1, c) for c in range(SUB)]
        down = [chosen(bits, [inv[r, c] if r >= c else zero for r in range(SUB)]) for c in range(SUB)]
        out.append(summed(down[c] * eus[c] for c in range(SUB)))
        if p == n - 1:
            break
        both = [chosen(bits, [full[max(r, c), min(r, c)] for r in range(SUB)]) for c in range(SUB)]
        v = summed(both[c] * get(SUB, c) for c in range(SUB))
        ve = summed(both[c] * eus[c] for c in range(SUB))
        get = rows_of([v, ve])
        lows = [spread(a[p + 1][:, SUB * p + c : SUB * p + c + 1]) for c in range(SUB)]
        a[p + 1] = a[p + 1] - summed(lows[c] * get(0, c) for c in range(SUB))
        e[p + 1] = e[p + 1] - summed(lows[c] * get(1, c) for c in range(SUB))
        if p + 2 < n:
            pieces = [jnp.zeros((p * SUB, 2 * LANES), F32)] if p else []
            pieces += [jnp.concatenate([v, ve], 1), jnp.zeros((LANES - (p + 1) * SUB, 2 * LANES), F32)]
            change = dot3(two_parts(jnp.concatenate(a[p + 2 :], 0)), two_parts(jnp.concatenate(pieces, 0)), NN)
            for i in range(p + 2, n):
                part = change[(i - p - 2) * SUB : (i - p - 1) * SUB]
                a[i] = a[i] - part[:, :LANES]
                e[i] = e[i] - part[:, LANES:]
    return jnp.concatenate(out, 0)


def sketch_kernel(parts, where_ref, map_ref, *refs):
    bonds, sites, refs = refs[:parts], refs[parts : parts + 2], refs[parts + 2 :]
    out_ref, site_ref, panels = refs[0], refs[1], refs[2 : parts + 2]
    rows_ref, site, high, low, sems = refs[parts + 2 :]
    legs, share, _ = site.shape
    size = bonds[0].shape[0]
    for k in range(2):

        @pl.when(where_ref[parts] == k)
        def _():
            site[...] = sites[k][...]

    copies = [pltpu.make_async_copy(site, site_ref, sems.at[parts])]
    copies[0].start()
    for n in range(parts):
        at = pl.ds(pl.multiple_of(where_ref[n] * size, size), size)
        sk = [dot1(bonds[n][...], site[u], NT) for u in range(legs)]
        for r in range(legs):
            total = summed(sk[u] * map_ref[at, u * legs + r : u * legs + r + 1] for u in range(legs))
            rows_ref[n, :, r * share : (r + 1) * share] = total
            hi, lo = two_parts(total)
            high[at, r * share : (r + 1) * share] = hi
            low[at, r * share : (r + 1) * share] = lo
        copies.append(pltpu.make_async_copy(rows_ref.at[n], out_ref.at[at, :], sems.at[n]))
        copies[-1].start()
    for j in range(parts):
        right = (high[j * size : (j + 1) * size, :], low[j * size : (j + 1) * size, :])
        panels[j][...] = dot3((high[j * size :, :], low[j * size :, :]), right, NT)
    for copy in copies:
        copy.wait()


def sketch(where, phys, bonds, sites):
    parts = len(bonds)
    size, width = bonds[0].shape
    legs, share, _ = sites[0].shape
    shapes = [jax.ShapeDtypeStruct((width, legs * share), F32), jax.ShapeDtypeStruct(sites[0].shape, BF16)]
    shapes += [jax.ShapeDtypeStruct((width - j * size, size), F32) for j in range(parts)]
    out = call(
        functools.partial(sketch_kernel, parts),
        "sketch",
        10e9,
        60,
        out_shape=shapes,
        in_specs=scalars(1) + whole(parts + 1 + len(sites)),
        out_specs=anywhere(2) + whole(parts),
        scratch_shapes=[
            VMEM((parts, size, legs * share), F32),
            VMEM(sites[0].shape, BF16),
            VMEM((width, legs * share), BF16),
            VMEM((width, legs * share), BF16),
            pltpu.SemaphoreType.DMA((parts + 1,)),
        ],
    )(where, phys, *bonds, *sites)
    return out[0], out[1], list(out[2:])


def basis_kernel(turn, groups, sums, last, *refs):
    sender, far_edges, refs = refs[0], refs[1:3], refs[3:]
    panels, refs = refs[:sums], refs[sums:]
    lows, refs = refs[:turn], refs[turn:]
    far_highs, refs = refs[: turn * groups], refs[turn * groups :]
    far_rests, refs = refs[:turn], refs[turn:]
    far_rows, refs = refs[:groups], refs[groups:]
    count = groups + (1 if last else 3)
    outs, refs = refs[:count], refs[count:]
    highs, rests, rows, edges, spots, sems = refs
    size = panels[0].shape[1]
    half = size // 2
    copies = []
    for g in range(groups):
        source = far_rows[g].at[turn * size : (turn + 1) * size, :]
        copies.append(pltpu.make_async_copy(source, rows.at[g], sems.at[g]))
    for i in range(turn):
        for g in range(groups):
            sem = sems.at[groups + i * (groups + 1) + g]
            copies.append(pltpu.make_async_copy(far_highs[i * groups + g], highs.at[i, g], sem))
        sem = sems.at[groups + i * (groups + 1) + groups]
        copies.append(pltpu.make_async_copy(far_rests[i], rests.at[i], sem))
    for k in range(2):
        source = far_edges[k].at[turn * size : (turn + 1) * size, :]
        copies.append(pltpu.make_async_copy(source, edges.at[k], sems.at[len(copies)]))
    for copy in copies:
        copy.start()
    s = summed(p[...] for p in panels)
    row = lax.broadcasted_iota(jnp.int32, s.shape, 0)
    lane = lax.broadcasted_iota(jnp.int32, s.shape, 1)
    s = s + jnp.where(row == lane, GRAM_SHIFT, 0.0).astype(F32)
    facing = []
    for i in range(turn):
        at = (turn - i - 1) * size
        below = two_parts(lows[i][at:, :])
        facing.append((below[0][:size], below[1][:size]))
        s = s - dot3(below, facing[i], NT)
    x1 = inverse_factor(s[:half, :half], spots.at[0])
    x1p = two_parts(x1)
    l21p = two_parts(dot3(two_parts(s[half:size, :half]), x1p, NT))
    x2 = inverse_factor(s[half:size, half:] - dot3(l21p, l21p, NT), spots.at[1])
    x2p = two_parts(x2)
    x21 = -dot3(x2p, two_parts(dot3(l21p, x1p, NN)), NN)
    inv = jnp.concatenate(
        [jnp.concatenate([x1, jnp.zeros((half, half), F32)], 1), jnp.concatenate([x21, x2], 1)], 0
    )
    inv = two_parts(inv)
    if not last:
        outs[groups + 2][...] = dot3(two_parts(s[size:, :]), inv, NT)
    for copy in copies:
        copy.wait()
    for g in range(groups):
        part = rows[g]
        for i in range(turn):
            part = part - dot3(facing[i], (highs[i, g], rests[i, g]), NN)
        hi, lo = two_parts(dot3(inv, two_parts(part), NN))
        outs[g][...] = hi
        if g == 0:
            outs[groups][...] = hi
        if not last:
            outs[groups + 1][g] = lo

    @pl.when(sender[0] == 1)
    def _():
        outs[groups][...] = edges[0]

    @pl.when(sender[0] == 2)
    def _():
        outs[groups][...] = edges[1]


def basis_columns(turn, sender, edges, panels, lows, highs, rests, rows):
    tall, size = panels[0].shape
    groups = len(rows)
    wide = rows[0].shape[1]
    last = tall == size
    shapes = [jax.ShapeDtypeStruct((size, wide), BF16)] * (groups + 1)
    if not last:
        shapes += [
            jax.ShapeDtypeStruct((groups, size, wide), BF16),
            jax.ShapeDtypeStruct((tall - size, size), F32),
        ]
    far = turn * (groups + 1) + groups
    return call(
        functools.partial(basis_kernel, turn, groups, len(panels), last),
        "basis",
        15e9,
        60,
        out_shape=shapes,
        in_specs=scalars(1) + anywhere(2) + whole(len(panels) + turn) + anywhere(far),
        out_specs=whole(len(shapes)),
        scratch_shapes=[
            VMEM((max(turn, 1), groups, size, wide), BF16),
            VMEM((max(turn, 1), groups, size, wide), BF16),
            VMEM((groups, size, wide), F32),
            VMEM((2, size, wide), BF16),
            VMEM((2, 12 * LANES, LANES), F32),
            pltpu.SemaphoreType.DMA((far + 2,)),
        ],
    )(sender, *edges, *panels, *lows, *[h for blocks in highs for h in blocks], *rests, *rows)


def absorb_kernel(legs, groups, more, mix_ref, *refs):
    bases, sites, (out_ref, held) = refs[: 2 * groups], refs[2 * groups : 4 * groups], refs[4 * groups + more :]
    size, wide = bases[0].shape
    share = wide // legs
    step = mix_ref.shape[0] // (legs * legs)
    for u in range(legs):
        for r in range(legs):
            at = slice(r * share, (r + 1) * share)
            total = summed(dot1(basis[:, at], site[u], NN) for basis, site in zip(bases, sites))
            held[u * legs + r] = total.astype(BF16)
    block = held.shape[2]
    for n in range(size // step):
        rows = slice(n * step, (n + 1) * step)
        stack = jnp.concatenate([held[m, rows, :] for m in range(legs * legs)], 0)
        mixed = dot1(mix_ref[...], stack, NN).astype(BF16)
        for d in range(legs):
            for l in range(legs):
                m = (d * legs + l) * step
                out_ref[0, d * size + n * step : d * size + (n + 1) * step, l * block : (l + 1) * block] = mixed[
                    m : m + step
                ]


def absorb(mix, bases, sites, first, count, *before):
    groups = len(bases) // 2
    size, wide = bases[0].shape
    legs, share, width = sites[0].shape
    parts = width // size
    site_spec = pl.BlockSpec((legs, share, size), lambda i: (0, 0, i + first))
    inputs = (mix, *bases, *sites, *before)
    return call(
        functools.partial(absorb_kernel, legs, groups, len(before)),
        "absorb",
        15e9 * count / parts,
        60,
        out_shape=jax.ShapeDtypeStruct((parts, legs * size, legs * size), BF16),
        grid=(count,),
        in_specs=whole(1 + len(bases)) + [site_spec] * len(sites) + anywhere(len(before)),
        out_specs=pl.BlockSpec((1, legs * size, legs * size), lambda i: (i + first, 0, 0)),
        scratch_shapes=[VMEM((legs * legs, size, size), BF16)],
        input_output_aliases={len(inputs) - 1: 0} if before else {},
    )(*inputs)


def close_kernel(parts, turns, legs, where_ref, weights, absorbed, *refs):
    lefts, (site_ref, transfer_ref, total) = refs[: parts * turns], refs[parts * turns :]
    n = pl.program_id(0)
    block = lefts[0].shape[0]

    @pl.when(n == 0)
    def _():
        total[...] = jnp.zeros_like(total)

    for i in range(parts):

        @pl.when(n == i)
        def _():
            for k in range(turns):
                total[:, k * block : (k + 1) * block] += dot1(absorbed[0], lefts[k * parts + i][...], NT)

    @pl.when(n == parts - 1)
    def _():
        size = transfer_ref.shape[0]
        terms = []
        for d in range(legs):
            part = total[d * size : (d + 1) * size, :].astype(BF16)
            site_ref[d] = part
            terms.append(part.astype(F32) * weights[d])
        transfer_ref[...] = summed(terms).astype(BF16)


def close(where, weights, absorbed, lefts):
    parts, tall, wide = absorbed.shape
    turns = len(lefts)
    legs = weights.shape[0]
    size, block = tall // legs, lefts[0][0].shape[0] * turns
    return call(
        functools.partial(close_kernel, parts, turns, legs),
        "close",
        3e9 * turns,
        60,
        out_shape=[
            jax.ShapeDtypeStruct((legs, size, block), BF16),
            jax.ShapeDtypeStruct((size, block), BF16),
        ],
        grid_spec=pltpu.PrefetchScalarGridSpec(
            num_scalar_prefetch=1,
            grid=(parts,),
            in_specs=scalars(1)
            + [pl.BlockSpec((1, tall, wide), lambda i, where: (where[i], 0, 0))]
            + whole(parts * turns),
            out_specs=whole(2),
            scratch_shapes=[VMEM((tall, block), F32)],
        ),
    )(where, weights, absorbed, *[piece for left in lefts for piece in left])


def settle_kernel(count, info, *refs):
    out = refs[2 * count]
    start = 0
    for n in range(count):
        wide = refs[2 * n].shape[2]
        for k in range(2):

            @pl.when(info[0] == k)
            def _(n=n, k=k, start=start, wide=wide):
                out[:, :, start : start + wide] = jnp.swapaxes(refs[2 * n + k][...], 0, 1)

        start += wide


def settle(kept, pairs):
    legs, size, _ = pairs[0][0].shape
    width = sum(p[0].shape[2] for p in pairs)
    return call(
        functools.partial(settle_kernel, len(pairs)),
        "settle",
        1e8,
        32,
        out_shape=jax.ShapeDtypeStruct((size, legs, width), BF16),
        in_specs=scalars(1) + whole(2 * len(pairs)),
        out_specs=pl.BlockSpec(memory_space=VMEM),
    )(kept, *[block for pair in pairs for block in pair])


def relay_kernel(parts, blocks, info, coming, kept, *refs):
    transfers, (out, weighted) = refs[: parts * blocks], refs[-2:]
    size, width = transfers[0].shape[0], kept.shape[1]
    whole_env = coming[...]
    first = whole_env.astype(BF16)
    left = whole_env - first.astype(F32)
    second = left.astype(BF16)
    third = (left - second.astype(F32)).astype(BF16)
    row = lax.broadcasted_iota(jnp.int32, (16, width), 0)
    grow = lambda v: jnp.broadcast_to(v.astype(F32), (16, width))
    lhs = jnp.where(row == 0, grow(first), jnp.where(row == 1, grow(second), jnp.where(row == 2, grow(third), 0.0)))
    lhs = lhs.astype(BF16)
    for n in range(parts):
        terms, start = [], 0
        for k in range(blocks):
            piece = transfers[n * blocks + k]
            terms.append(dot1(lhs[:, start : start + piece.shape[1]], piece[...], NT))
            start += piece.shape[1]
        product = summed(terms)
        at = pl.ds(pl.multiple_of(info[n] * size, size), size)
        weighted[:, at] = jnp.sum(product, axis=0, keepdims=True)
    w = weighted[...]
    squares = jnp.sum(w * w, axis=1, keepdims=True)
    env = w * jnp.sqrt(jnp.float32(width)) / jnp.sqrt(squares + 1e-06)
    out[...] = jnp.where(info[parts] == 1, env, kept[...])


def relay(info, coming, kept, transfers, *riders):
    parts, blocks = len(transfers), len(transfers[0])
    return call(
        functools.partial(relay_kernel, parts, blocks),
        "relay",
        1e8,
        24,
        out_shape=jax.ShapeDtypeStruct(kept.shape, F32),
        in_specs=scalars(1) + whole(2 + parts * blocks) + anywhere(len(riders)),
        out_specs=pl.BlockSpec(memory_space=VMEM),
        scratch_shapes=[VMEM(kept.shape, F32)],
    )(info, coming, kept, *[piece for blocks_of in transfers for piece in blocks_of], *riders)


def paired(columns, tiles, boundary, row_tensors, sketch_bond, sketch_phys, edge_factor, closing, left_edge):
    planes, rows = columns // 2, tiles // 2

    def number(z, c, y, x):
        return (2 * z + c) * tiles + 2 * y + x

    every = [(z, c, y, x) for z in range(planes) for c in range(2) for y in range(rows) for x in range(2)]

    def which(z, x):
        return x ^ (z & 1)

    def fetch(i):
        return [
            (number(z, which(z, x), (y + i) % rows, x ^ c ^ (i & 1)), number(z, c, y, x)) for z, c, y, x in every
        ]

    home = [(b, a) for a, b in fetch(0)]
    core = [(number(z, c, y, x), number(z, 1 - c, y, x)) for z, c, y, x in every]
    cross = [(number(z, c, y, x), number(z, c, y, 1 - x)) for z, c, y, x in every]

    def turned(i):
        return [(number(z, c, (y + i) % rows, x), number(z, c, y, x)) for z, c, y, x in every]

    def right_of(z, c, y, x):
        if which(z, x) == 0:
            return number(z, c, y, 1 - x)
        return number(z + 1, c, y, x) if z + 1 < planes else None

    right = [
        (number(z, c, y, x), number(0, c, y, 0) if right_of(z, c, y, x) is None else right_of(z, c, y, x))
        for z, c, y, x in every
    ]
    end = which(planes - 1, 1)
    edge_route = [
        (number(planes - 1, c, y, 1 - end), number(planes - 1, c, y, end)) for y in range(rows) for c in (1 - end,)
    ]

    def move(block, route):
        return lax.ppermute(block, AXES, route)

    def move_or_keep(block, route):
        keeps = [a for a, b in route if a == b]
        moved = move(block, [(a, b) for a, b in route if a != b])
        return jnp.where(functools.reduce(jnp.logical_or, [me == a for a in keeps], me < 0), block, moved)

    col, tile = lax.axis_index("col"), lax.axis_index("tile")
    z, c, y, x = col // 2, col % 2, tile // 2, tile % 2
    s = (x + z) % 2
    site_number = 2 * z + s
    me = col * tiles + tile
    own_column = c == s

    share, legs, width = boundary.shape[1:]
    size = width // tiles

    small = jnp.concatenate(
        [
            sketch_phys[0].reshape(legs * legs, width).astype(F32),
            jnp.pad(
                jnp.concatenate([row_tensors[0].reshape(-1).astype(F32), closing[0]]),
                (0, width - legs**4 - legs),
            )[None],
        ]
    )
    small = jnp.where(own_column, small, move(small, core))
    row_tensor = small[-1, : legs**4].reshape(legs, legs, legs, legs)
    weights = small[-1, legs**4 : legs**4 + legs]
    phys_map = jnp.einsum(
        "lurd,ldk->kur",
        row_tensor,
        small[:-1].reshape(legs, legs, width),
        precision=lax.Precision.HIGHEST,
    ).reshape(width, legs * legs)
    step = size // (legs * legs)
    mix = jnp.einsum("lurd,ab->dlaurb", row_tensor, jnp.eye(step, dtype=F32))
    mix = mix.reshape(legs * legs * step, legs * legs * step).astype(BF16)

    ahead = jnp.arange(rows, dtype=jnp.int32)
    near = 2 * ((y + ahead) % rows) + (x + c + ahead) % 2
    far = 2 * ((y + ahead) % rows) + (x + c + ahead + 1) % 2
    spots = jnp.concatenate([near, far]).astype(jnp.int32)

    def after(value, *earlier):
        return lax.optimization_barrier((value, *earlier))[0]

    bonds = [move_or_keep(sketch_bond[0], fetch(i)) for i in range(rows)]
    site = after(boundary[0].transpose(1, 0, 2), *bonds)
    edge = after(edge_factor, bonds[-1]).transpose(2, 1, 0).reshape(width, legs * share)
    phys_map, mix, edge = lax.optimization_barrier((phys_map, mix, edge))
    near_site = move(site, [(a, b) for a, b in fetch(0) if a != b])
    keep = functools.reduce(jnp.logical_or, [me == a for a, b in fetch(0) if a == b], me < 0)
    choices = [(near_site, site)]
    flags = [keep.astype(jnp.int32)]
    second = [[(a, b) for a, b in fetch(i) if (b // tiles) % 2 == 1] for i in range(1, rows)]
    direct = [move(site, route) for route in second]
    for i in range(1, rows):
        route = [(a, b) for a, b in fetch(i) if (b // tiles) % 2 == 0]
        choices.append((move(after(site, near_site, *direct, edge, phys_map, mix), route), direct[i - 1]))
        flags.append(c.astype(jnp.int32))
    arrived = choices[-1][0]
    bonds += [move(b, core) for b in bonds]

    range_rows, panels, sites = [], [], []
    for choice, flag in zip(choices, flags):
        if panels:
            choice = (after(choice[0], panels[-1][0]), choice[1])
        rows_t, chosen_site, own = sketch(jnp.concatenate([spots, flag[None]]), phys_map, bonds, choice)
        range_rows.append(rows_t)
        sites.append(chosen_site)
        panels.append(own)
    others = [[move(p, core) for p in own] for own in panels[:-1]]
    first = move(panels[-1][0], core)
    others.append([first] + [move(after(p, first), core) for p in panels[-1][1:]])
    all_panels = [[own[turn] for own in panels + others] for turn in range(tiles)]
    sites += [move(after(b, *others[-1]), core) for b in sites]

    edges = [edge, move(after(edge, arrived), edge_route)]
    sender = jnp.where(site_number == columns - 1, jnp.where(c == x, 1, 2), 0).astype(jnp.int32)[None]

    lows, highs, rests, comes, turns, swaps = [], [], [], [], [], []

    def turn_round(come):
        return [move(come, turned(i)) for i in range(1, rows)]

    def swap(blocks):
        return [move(b, core) for b in blocks]

    for turn in range(tiles):
        parts = all_panels[turn]
        if turn >= 2:
            past = [comes[turn - 2]] + (turns[turn - 3] + swaps[turn - 3][:1] if turn >= 3 else [])
            parts = [after(parts[0], *past)] + parts[1:]
            if turn >= 3:
                swaps[turn - 3] += swap(turns[turn - 3])
            turns.append(turn_round(comes[turn - 2]))
            swaps.append(swap(comes[turn - 2 : turn - 1]))
        out = basis_columns(turn, sender, edges, parts, lows, highs, rests, range_rows)
        highs.append(out[:rows])
        comes.append(move(out[rows], right))
        if turn < tiles - 1:
            rests.append(out[rows + 1])
            lows.append(out[rows + 2])

    def picked(q):
        out = list(highs[0])
        for turn in range(1, tiles):
            out = [jnp.where(q == turn, new, old) for new, old in zip(highs[turn], out)]
        return out

    basis_b = [move(b, core) for b in picked(far[0])]
    basis_a = picked(near[0])
    basis_a[0] = after(basis_a[0], *[b for blocks in swaps for b in blocks], *turns[-1])
    turns.append(turn_round(comes[-2]))
    swaps.append(swap(comes[-2:-1]))
    absorbed = absorb(mix, basis_a + basis_b, sites, 0, tiles // 2)
    mix, comes[-1], absorbed, turns[-2], turns[-1], swaps[-1] = lax.optimization_barrier(
        (mix, comes[-1], absorbed, turns[-2], turns[-1], swaps[-1])
    )
    come = comes[-1]
    swaps[-2] += swap(turns[-2])
    swaps[-1] += swap(turns[-1])
    turns.append(turn_round(come))
    swaps.append(swap([come]))
    absorbed = absorb(mix, basis_a + basis_b, sites, tiles // 2, tiles - tiles // 2, absorbed)
    absorbed, last, _ = lax.optimization_barrier((absorbed, turns[-1], swaps))
    swaps[-1] += swap(last)
    lefts = [[come] + blocks + others_ for come, blocks, others_ in zip(comes, turns, swaps)]

    source = jnp.where(s == 1, 1 - x, x)
    near_left = 2 * ((y + ahead) % rows) + (source + c) % 2
    far_left = 2 * ((y + ahead) % rows) + (source + c + 1) % 2
    left_spots = jnp.concatenate([near_left, far_left]).astype(jnp.int32)
    near_own = 2 * ((y + ahead) % rows) + (x + c) % 2
    far_own = 2 * ((y + ahead) % rows) + (x + c + 1) % 2
    own_spots = jnp.concatenate([near_own, far_own]).astype(jnp.int32)

    new_early, transfer_early = close(left_spots, weights, absorbed, lefts[:-1])
    transfer_early = [transfer_early] + [move(transfer_early, turned(i)) for i in range(1, rows)]
    home_moves = [(a, b) for a, b in home if a != b]
    home_early = move(new_early, home_moves)
    new_late, transfer_late = close(left_spots, weights, after(absorbed, transfer_early[0]), lefts[-1:])
    other_core = dict(core)
    routes = [turned(i) for i in range(1, rows)]
    routes += [core] + [[(a, other_core[b]) for a, b in turned(i)] for i in range(1, rows)]
    transfer_early += swap([after(t, transfer_late) for t in transfer_early])
    transfer_late = [transfer_late] + [move(transfer_late, route) for route in routes]
    transfers = [list(pair) for pair in zip(transfer_early, transfer_late)]

    starts = [d for d in every if right_of(*d) is not None]
    kept = left_edge[None]
    for turn in range(columns):
        env = kept
        if turn:
            route = [(number(*d), right_of(*d)) for d in starts if 2 * d[0] + which(d[0], d[3]) == turn - 1]
            env = move(kept, route)
        info = jnp.concatenate([own_spots, (site_number == turn).astype(jnp.int32)[None]])
        riders = []
        if turn == 2:
            home_late = move(after(new_late, kept), home_moves)
        if turn == columns // 2 + 1:
            stays = functools.reduce(jnp.logical_or, [me == a for a, b in home if a == b], me < 0)
            new_site = settle(
                (1 - stays.astype(jnp.int32))[None], [(new_early, home_early), (new_late, home_late)]
            )
            riders = [new_site]
        kept = relay(info, env, kept, transfers, *riders)
    env = jnp.where(own_column, kept, move(kept, cross))
    env = lax.dynamic_slice_in_dim(env, tile * share, share, axis=1)
    return new_site[None], env


def solution(mesh):
    in_specs = (
        P("col", "tile", None, None),
        P("col", None, None, None, None),
        P("col", "tile", None),
        P("col", None, None, None),
        P("tile", None, None),
        P("col", None),
        P(),
    )
    out_specs = (P("col", "tile", None, None), P("col", "tile"))
    columns, tiles = mesh.shape["col"], mesh.shape["tile"]

    def local(*args):
        share, legs, width = args[0].shape[1:]
        even = columns % 2 == 0 and tiles % 2 == 0
        if even and share % (2 * LANES) == 0 and share == width // tiles and legs**4 + legs <= width:
            return paired(columns, tiles, *args)
        return plain(*args)

    return jax.shard_map(local, mesh=mesh, in_specs=in_specs, out_specs=out_specs, check_vma=False)
```

```python
import functools

import jax
import jax.numpy as jnp
from jax import lax
from jax.experimental import pallas as pl
from jax.experimental.pallas import tpu as pltpu
from jax.sharding import PartitionSpec as P

GRAM_SHIFT = 0.001
F32 = jnp.float32
BF16 = jnp.bfloat16
LANES = 128
SUB = 8
VMEM = pltpu.VMEM
NT = ((1,), (1,))
NN = ((1,), (0,))
AXES = ("col", "tile")


def passed_along(block, axis, distance):
    devices = range(lax.axis_size(axis))
    route = [(i - distance, i) for i in devices if i - distance in devices]
    return lax.ppermute(block, axis, route)


def plain(boundary, row_tensors, sketch_bond, sketch_phys, edge_factor, closing, left_edge):
    highest = lax.Precision.HIGHEST
    own_site = boundary[0]
    row_tensor = row_tensors[0].astype(jnp.float32)
    bond_sketch = sketch_bond[0]
    phys_map = jnp.einsum(
        "lurd,ldk->urk", row_tensor, sketch_phys[0].astype(jnp.float32), precision=highest
    )
    local_rows = own_site.shape[0]
    legs = own_site.shape[1]
    width = own_site.shape[2]
    sketched = jnp.einsum(
        "bua,ka->buk",
        own_site,
        lax.all_gather(bond_sketch, "tile", axis=0, tiled=True),
        preferred_element_type=jnp.float32,
    )
    range_rows = jnp.sum(sketched[:, :, None, :] * phys_map[None], axis=1)
    range_flat = range_rows.reshape(local_rows * legs, width)
    gram_local = jnp.dot(range_flat.T, range_flat, precision=highest)
    gram_total = lax.psum(gram_local, "tile") + GRAM_SHIFT * jnp.eye(width, dtype=jnp.float32)
    lower_factor = jnp.linalg.cholesky(gram_total)
    basis = jax.scipy.linalg.solve_triangular(lower_factor, range_flat.T, lower=True).T
    basis = basis.astype(jnp.bfloat16).reshape(local_rows, legs, width)
    arrived = passed_along(basis, "col", 1)
    first_column = lax.axis_index("col") == 0
    left_basis = jnp.where(first_column, edge_factor, arrived)
    basis_cols = lax.all_to_all(basis, "tile", split_axis=2, concat_axis=0, tiled=True)
    matching = basis_cols
    right_part = jnp.einsum(
        "bua,brk->aurk",
        lax.all_gather(own_site, "tile", axis=0, tiled=True),
        matching,
        preferred_element_type=jnp.float32,
    )
    absorbed = jnp.einsum("aurk,lurd->aldk", right_part, row_tensor, precision=highest)
    matching = absorbed
    new_site = jnp.einsum(
        "alc,aldk->kdc",
        lax.all_gather(left_basis, "tile", axis=0, tiled=True).astype(jnp.float32),
        matching,
        precision=highest,
    )
    new_site = new_site.astype(jnp.bfloat16)
    transfer_rows = jnp.einsum(
        "kdc,d->kc", new_site.astype(jnp.float32), closing[0], precision=highest
    ).astype(jnp.bfloat16)
    scale = jnp.sqrt(jnp.float32(width))
    column_count = lax.axis_size("col")
    share = transfer_rows.shape[0]
    transfer_local = transfer_rows.astype(jnp.float32)

    def relay_split(turn_index, current):
        incoming = passed_along(current, "col", 1)
        incoming_whole = lax.all_gather(incoming, "tile", axis=0, tiled=True)
        incoming_whole = jnp.where(first_column, left_edge, incoming_whole)
        weighted = jnp.dot(transfer_local, incoming_whole, precision=highest)
        squares = lax.psum(jnp.sum(weighted * weighted), "tile")
        return weighted * scale / jnp.sqrt(squares + 1e-06)

    env_local = lax.fori_loop(0, column_count, relay_split, jnp.zeros((share,), jnp.float32))
    return (new_site[None], env_local[None])


def call(kernel, name, flops, vmem, **kwargs):
    return pl.pallas_call(
        kernel,
        name=name,
        compiler_params=pltpu.CompilerParams(vmem_limit_bytes=vmem * 2**20),
        cost_estimate=pl.CostEstimate(flops=int(flops), bytes_accessed=1 << 20, transcendentals=0),
        **kwargs,
    )


def whole(count):
    return [pl.BlockSpec(memory_space=VMEM)] * count


def anywhere(count):
    return [pl.BlockSpec(memory_space=pl.ANY)] * count


def scalars(count):
    return [pl.BlockSpec(memory_space=pltpu.SMEM)] * count


def two_parts(x):
    hi = x.astype(BF16)
    return hi, (x - hi.astype(F32)).astype(BF16)


def dot1(a, b, dims):
    return lax.dot_general(a, b, (dims, ((), ())), preferred_element_type=F32)


def dot3(a, b, dims):
    (ah, al), (bh, bl) = a, b
    return dot1(ah, bh, dims) + (dot1(ah, bl, dims) + dot1(al, bh, dims))


def spread(x):
    return jnp.broadcast_to(x, (SUB, LANES))


def summed(terms):
    terms = list(terms)
    while len(terms) > 1:
        terms = [terms[i] + terms[i + 1] if i + 1 < len(terms) else terms[i] for i in range(0, len(terms), 2)]
    return terms[0]


def chosen(bits, entries):
    entries = list(entries)
    for bit in bits:
        entries = [
            entries[i] if entries[i] is entries[i + 1] else jnp.where(bit, entries[i + 1], entries[i])
            for i in range(0, len(entries), 2)
        ]
    return entries[0]


def factor_panel(s):
    s = dict(s)
    inv = {}
    full = {}
    for c in range(SUB):
        rs = lax.rsqrt(s[c, c])
        low = {r: s[r, c] * rs for r in range(c + 1, SUB)}
        for r in range(c + 1, SUB):
            for q in range(c + 1, r + 1):
                s[r, q] = s[r, q] - low[r] * low[q]
        for q in range(c):
            inv[c, q] = inv[c, q] * rs
        inv[c, c] = rs
        for r in range(c + 1, SUB):
            for q in range(c + 1):
                term = low[r] * inv[c, q]
                inv[r, q] = inv[r, q] - term if (r, q) in inv else -term
        for r in range(c + 1):
            for q in range(r + 1):
                term = inv[c, r] * inv[c, q]
                full[r, q] = full[r, q] + term if (r, q) in full else term
    return inv, full


def inverse_factor(block, scratch):
    n = LANES // SUB
    row = lax.broadcasted_iota(jnp.int32, (SUB, LANES), 0)
    lane = lax.broadcasted_iota(jnp.int32, (SUB, LANES), 1)
    bits = [(row & b) != 0 for b in (1, 2, 4)]
    zero = jnp.zeros((SUB, LANES), F32)
    a = [block[SUB * i : SUB * (i + 1), :] for i in range(n)]
    e = [jnp.where(lane == row + SUB * i, 1.0, 0.0).astype(F32) for i in range(n)]
    used = 0

    def rows_of(registers):
        nonlocal used
        base, used = used, used + len(registers)
        for k, register in enumerate(registers):
            scratch[(base + k) * SUB : (base + k + 1) * SUB, :] = register
        return lambda k, r: scratch[pl.ds((base + k) * SUB + r, SUB, stride=0), :]

    out = []
    for p in range(n):
        u, eu = a[p], e[p]
        get = rows_of([spread(u[:, SUB * p + c : SUB * p + c + 1]) for c in range(SUB)] + [u, eu])
        inv, full = factor_panel({(r, c): get(c, r) for c in range(SUB) for r in range(c, SUB)})
        eus = [get(SUB + 1, c) for c in range(SUB)]
        down = [chosen(bits, [inv[r, c] if r >= c else zero for r in range(SUB)]) for c in range(SUB)]
        out.append(summed(down[c] * eus[c] for c in range(SUB)))
        if p == n - 1:
            break
        both = [chosen(bits, [full[max(r, c), min(r, c)] for r in range(SUB)]) for c in range(SUB)]
        v = summed(both[c] * get(SUB, c) for c in range(SUB))
        ve = summed(both[c] * eus[c] for c in range(SUB))
        get = rows_of([v, ve])
        lows = [spread(a[p + 1][:, SUB * p + c : SUB * p + c + 1]) for c in range(SUB)]
        a[p + 1] = a[p + 1] - summed(lows[c] * get(0, c) for c in range(SUB))
        e[p + 1] = e[p + 1] - summed(lows[c] * get(1, c) for c in range(SUB))
        if p + 2 < n:
            pieces = [jnp.zeros((p * SUB, 2 * LANES), F32)] if p else []
            pieces += [jnp.concatenate([v, ve], 1), jnp.zeros((LANES - (p + 1) * SUB, 2 * LANES), F32)]
            change = dot3(two_parts(jnp.concatenate(a[p + 2 :], 0)), two_parts(jnp.concatenate(pieces, 0)), NN)
            for i in range(p + 2, n):
                part = change[(i - p - 2) * SUB : (i - p - 1) * SUB]
                a[i] = a[i] - part[:, :LANES]
                e[i] = e[i] - part[:, LANES:]
    return jnp.concatenate(out, 0)


def sketch_kernel(parts, where_ref, map_ref, *refs):
    bonds, sites, refs = refs[:parts], refs[parts : parts + 2], refs[parts + 2 :]
    out_ref, site_ref, panels = refs[0], refs[1], refs[2 : parts + 2]
    rows_ref, site, high, low, sems = refs[parts + 2 :]
    legs, share, _ = site.shape
    size = bonds[0].shape[0]
    for k in range(2):

        @pl.when(where_ref[parts] == k)
        def _():
            site[...] = sites[k][...]

    copies = [pltpu.make_async_copy(site, site_ref, sems.at[parts])]
    copies[0].start()
    for n in range(parts):
        at = pl.ds(pl.multiple_of(where_ref[n] * size, size), size)
        sk = [dot1(bonds[n][...], site[u], NT) for u in range(legs)]
        for r in range(legs):
            total = summed(sk[u] * map_ref[at, u * legs + r : u * legs + r + 1] for u in range(legs))
            rows_ref[n, :, r * share : (r + 1) * share] = total
            hi, lo = two_parts(total)
            high[at, r * share : (r + 1) * share] = hi
            low[at, r * share : (r + 1) * share] = lo
        copies.append(pltpu.make_async_copy(rows_ref.at[n], out_ref.at[at, :], sems.at[n]))
        copies[-1].start()
    for j in range(parts):
        right = (high[j * size : (j + 1) * size, :], low[j * size : (j + 1) * size, :])
        panels[j][...] = dot3((high[j * size :, :], low[j * size :, :]), right, NT)
    for copy in copies:
        copy.wait()


def sketch(where, phys, bonds, sites):
    parts = len(bonds)
    size, width = bonds[0].shape
    legs, share, _ = sites[0].shape
    shapes = [jax.ShapeDtypeStruct((width, legs * share), F32), jax.ShapeDtypeStruct(sites[0].shape, BF16)]
    shapes += [jax.ShapeDtypeStruct((width - j * size, size), F32) for j in range(parts)]
    out = call(
        functools.partial(sketch_kernel, parts),
        "sketch",
        10e9,
        60,
        out_shape=shapes,
        in_specs=scalars(1) + whole(parts + 1 + len(sites)),
        out_specs=anywhere(2) + whole(parts),
        scratch_shapes=[
            VMEM((parts, size, legs * share), F32),
            VMEM(sites[0].shape, BF16),
            VMEM((width, legs * share), BF16),
            VMEM((width, legs * share), BF16),
            pltpu.SemaphoreType.DMA((parts + 1,)),
        ],
    )(where, phys, *bonds, *sites)
    return out[0], out[1], list(out[2:])


def basis_kernel(turn, groups, sums, last, *refs):
    sender, far_edges, refs = refs[0], refs[1:3], refs[3:]
    panels, refs = refs[:sums], refs[sums:]
    lows, refs = refs[:turn], refs[turn:]
    far_highs, refs = refs[: turn * groups], refs[turn * groups :]
    far_rests, refs = refs[:turn], refs[turn:]
    far_rows, refs = refs[:groups], refs[groups:]
    count = groups + (1 if last else 3)
    outs, refs = refs[:count], refs[count:]
    highs, rests, rows, edges, spots, sems = refs
    size = panels[0].shape[1]
    half = size // 2
    copies = []
    for g in range(groups):
        source = far_rows[g].at[turn * size : (turn + 1) * size, :]
        copies.append(pltpu.make_async_copy(source, rows.at[g], sems.at[g]))
    for i in range(turn):
        for g in range(groups):
            sem = sems.at[groups + i * (groups + 1) + g]
            copies.append(pltpu.make_async_copy(far_highs[i * groups + g], highs.at[i, g], sem))
        sem = sems.at[groups + i * (groups + 1) + groups]
        copies.append(pltpu.make_async_copy(far_rests[i], rests.at[i], sem))
    for k in range(2):
        source = far_edges[k].at[turn * size : (turn + 1) * size, :]
        copies.append(pltpu.make_async_copy(source, edges.at[k], sems.at[len(copies)]))
    for copy in copies:
        copy.start()
    s = summed(p[...] for p in panels)
    row = lax.broadcasted_iota(jnp.int32, s.shape, 0)
    lane = lax.broadcasted_iota(jnp.int32, s.shape, 1)
    s = s + jnp.where(row == lane, GRAM_SHIFT, 0.0).astype(F32)
    facing = []
    for i in range(turn):
        at = (turn - i - 1) * size
        below = two_parts(lows[i][at:, :])
        facing.append((below[0][:size], below[1][:size]))
        s = s - dot3(below, facing[i], NT)
    x1 = inverse_factor(s[:half, :half], spots.at[0])
    x1p = two_parts(x1)
    l21p = two_parts(dot3(two_parts(s[half:size, :half]), x1p, NT))
    x2 = inverse_factor(s[half:size, half:] - dot3(l21p, l21p, NT), spots.at[1])
    x2p = two_parts(x2)
    x21 = -dot3(x2p, two_parts(dot3(l21p, x1p, NN)), NN)
    inv = jnp.concatenate(
        [jnp.concatenate([x1, jnp.zeros((half, half), F32)], 1), jnp.concatenate([x21, x2], 1)], 0
    )
    inv = two_parts(inv)
    if not last:
        outs[groups + 2][...] = dot3(two_parts(s[size:, :]), inv, NT)
    for copy in copies:
        copy.wait()
    for g in range(groups):
        part = rows[g]
        for i in range(turn):
            part = part - dot3(facing[i], (highs[i, g], rests[i, g]), NN)
        hi, lo = two_parts(dot3(inv, two_parts(part), NN))
        outs[g][...] = hi
        if g == 0:
            outs[groups][...] = hi
        if not last:
            outs[groups + 1][g] = lo

    @pl.when(sender[0] == 1)
    def _():
        outs[groups][...] = edges[0]

    @pl.when(sender[0] == 2)
    def _():
        outs[groups][...] = edges[1]


def basis_columns(turn, sender, edges, panels, lows, highs, rests, rows):
    tall, size = panels[0].shape
    groups = len(rows)
    wide = rows[0].shape[1]
    last = tall == size
    shapes = [jax.ShapeDtypeStruct((size, wide), BF16)] * (groups + 1)
    if not last:
        shapes += [
            jax.ShapeDtypeStruct((groups, size, wide), BF16),
            jax.ShapeDtypeStruct((tall - size, size), F32),
        ]
    far = turn * (groups + 1) + groups
    return call(
        functools.partial(basis_kernel, turn, groups, len(panels), last),
        "basis",
        15e9,
        60,
        out_shape=shapes,
        in_specs=scalars(1) + anywhere(2) + whole(len(panels) + turn) + anywhere(far),
        out_specs=whole(len(shapes)),
        scratch_shapes=[
            VMEM((max(turn, 1), groups, size, wide), BF16),
            VMEM((max(turn, 1), groups, size, wide), BF16),
            VMEM((groups, size, wide), F32),
            VMEM((2, size, wide), BF16),
            VMEM((2, 12 * LANES, LANES), F32),
            pltpu.SemaphoreType.DMA((far + 2,)),
        ],
    )(sender, *edges, *panels, *lows, *[h for blocks in highs for h in blocks], *rests, *rows)


def absorb_kernel(legs, groups, more, mix_ref, *refs):
    bases, sites, (out_ref, held) = refs[: 2 * groups], refs[2 * groups : 4 * groups], refs[4 * groups + more :]
    size, wide = bases[0].shape
    share = wide // legs
    step = mix_ref.shape[0] // (legs * legs)
    for u in range(legs):
        for r in range(legs):
            at = slice(r * share, (r + 1) * share)
            total = summed(dot1(basis[:, at], site[u], NN) for basis, site in zip(bases, sites))
            held[u * legs + r] = total.astype(BF16)
    block = held.shape[2]
    for n in range(size // step):
        rows = slice(n * step, (n + 1) * step)
        stack = jnp.concatenate([held[m, rows, :] for m in range(legs * legs)], 0)
        mixed = dot1(mix_ref[...], stack, NN).astype(BF16)
        for d in range(legs):
            for l in range(legs):
                m = (d * legs + l) * step
                out_ref[0, d * size + n * step : d * size + (n + 1) * step, l * block : (l + 1) * block] = mixed[
                    m : m + step
                ]


def absorb(mix, bases, sites, first, count, *before):
    groups = len(bases) // 2
    size, wide = bases[0].shape
    legs, share, width = sites[0].shape
    parts = width // size
    site_spec = pl.BlockSpec((legs, share, size), lambda i: (0, 0, i + first))
    inputs = (mix, *bases, *sites, *before)
    return call(
        functools.partial(absorb_kernel, legs, groups, len(before)),
        "absorb",
        15e9 * count / parts,
        60,
        out_shape=jax.ShapeDtypeStruct((parts, legs * size, legs * size), BF16),
        grid=(count,),
        in_specs=whole(1 + len(bases)) + [site_spec] * len(sites) + anywhere(len(before)),
        out_specs=pl.BlockSpec((1, legs * size, legs * size), lambda i: (i + first, 0, 0)),
        scratch_shapes=[VMEM((legs * legs, size, size), BF16)],
        input_output_aliases={len(inputs) - 1: 0} if before else {},
    )(*inputs)


def close_kernel(parts, turns, legs, more, where_ref, weights, absorbed, *refs):
    lefts, (site_ref, transfer_ref, total) = refs[: parts * turns], refs[parts * turns + more :]
    n = pl.program_id(0)
    block = lefts[0].shape[0]

    @pl.when(n == 0)
    def _():
        total[...] = jnp.zeros_like(total)

    for i in range(parts):

        @pl.when(n == i)
        def _():
            for k in range(turns):
                total[:, k * block : (k + 1) * block] += dot1(absorbed[0], lefts[k * parts + i][...], NT)

    @pl.when(n == parts - 1)
    def _():
        size = transfer_ref.shape[0]
        terms = []
        for d in range(legs):
            part = total[d * size : (d + 1) * size, :].astype(BF16)
            site_ref[d] = part
            terms.append(part.astype(F32) * weights[d])
        transfer_ref[...] = summed(terms).astype(BF16)


def close(where, weights, absorbed, lefts, first, *before):
    parts, tall, wide = absorbed.shape
    turns = len(lefts)
    legs = weights.shape[0]
    size, block = tall // legs, lefts[0][0].shape[0] * turns
    inputs = (where, weights, absorbed, *[piece for left in lefts for piece in left], *before)
    return call(
        functools.partial(close_kernel, parts, turns, legs, len(before)),
        "close",
        3e9 * turns,
        60,
        out_shape=[
            jax.ShapeDtypeStruct((legs, size, size * parts), BF16),
            jax.ShapeDtypeStruct((size, block), BF16),
        ],
        grid_spec=pltpu.PrefetchScalarGridSpec(
            num_scalar_prefetch=1,
            grid=(parts,),
            in_specs=scalars(1)
            + [pl.BlockSpec((1, tall, wide), lambda i, where: (where[i], 0, 0))]
            + whole(parts * turns)
            + anywhere(len(before)),
            out_specs=[pl.BlockSpec((legs, size, block), lambda i, where: (0, 0, first * size // block))] + whole(1),
            scratch_shapes=[VMEM((tall, block), F32)],
        ),
        input_output_aliases={len(inputs) - 1: 0} if before else {},
    )(*inputs)


def settle_kernel(count, info, *refs):
    out = refs[2 * count]
    start = 0
    for n in range(count):
        wide = refs[2 * n].shape[2]
        for k in range(2):

            @pl.when(info[0] == k)
            def _(n=n, k=k, start=start, wide=wide):
                out[:, :, start : start + wide] = jnp.swapaxes(refs[2 * n + k][...], 0, 1)

        start += wide


def settle(kept, pairs):
    legs, size, _ = pairs[0][0].shape
    width = sum(p[0].shape[2] for p in pairs)
    return call(
        functools.partial(settle_kernel, len(pairs)),
        "settle",
        1e8,
        32,
        out_shape=jax.ShapeDtypeStruct((size, legs, width), BF16),
        in_specs=scalars(1) + whole(2 * len(pairs)),
        out_specs=pl.BlockSpec(memory_space=VMEM),
    )(kept, *[block for pair in pairs for block in pair])


def relay_kernel(parts, blocks, info, coming, kept, *refs):
    transfers, (out, weighted) = refs[: parts * blocks], refs[-2:]
    size, width = transfers[0].shape[0], kept.shape[1]
    whole_env = coming[...]
    first = whole_env.astype(BF16)
    left = whole_env - first.astype(F32)
    second = left.astype(BF16)
    third = (left - second.astype(F32)).astype(BF16)
    row = lax.broadcasted_iota(jnp.int32, (16, width), 0)
    grow = lambda v: jnp.broadcast_to(v.astype(F32), (16, width))
    lhs = jnp.where(row == 0, grow(first), jnp.where(row == 1, grow(second), jnp.where(row == 2, grow(third), 0.0)))
    lhs = lhs.astype(BF16)
    for n in range(parts):
        terms, start = [], 0
        for k in range(blocks):
            piece = transfers[n * blocks + k]
            terms.append(dot1(lhs[:, start : start + piece.shape[1]], piece[...], NT))
            start += piece.shape[1]
        product = summed(terms)
        at = pl.ds(pl.multiple_of(info[n] * size, size), size)
        weighted[:, at] = jnp.sum(product, axis=0, keepdims=True)
    w = weighted[...]
    squares = jnp.sum(w * w, axis=1, keepdims=True)
    env = w * jnp.sqrt(jnp.float32(width)) / jnp.sqrt(squares + 1e-06)
    out[...] = jnp.where(info[parts] == 1, env, kept[...])


def relay(info, coming, kept, transfers, *riders):
    parts, blocks = len(transfers), len(transfers[0])
    return call(
        functools.partial(relay_kernel, parts, blocks),
        "relay",
        1e8,
        24,
        out_shape=jax.ShapeDtypeStruct(kept.shape, F32),
        in_specs=scalars(1) + whole(2 + parts * blocks) + anywhere(len(riders)),
        out_specs=pl.BlockSpec(memory_space=VMEM),
        scratch_shapes=[VMEM(kept.shape, F32)],
    )(info, coming, kept, *[piece for blocks_of in transfers for piece in blocks_of], *riders)


def paired(columns, tiles, boundary, row_tensors, sketch_bond, sketch_phys, edge_factor, closing, left_edge):
    planes, rows = columns // 2, tiles // 2

    def number(z, c, y, x):
        return (2 * z + c) * tiles + 2 * y + x

    every = [(z, c, y, x) for z in range(planes) for c in range(2) for y in range(rows) for x in range(2)]

    def which(z, x):
        return x ^ (z & 1)

    def fetch(i):
        return [
            (number(z, which(z, x), (y + i) % rows, x ^ c ^ (i & 1)), number(z, c, y, x)) for z, c, y, x in every
        ]

    home = [(b, a) for a, b in fetch(0)]
    core = [(number(z, c, y, x), number(z, 1 - c, y, x)) for z, c, y, x in every]
    cross = [(number(z, c, y, x), number(z, c, y, 1 - x)) for z, c, y, x in every]

    def turned(i):
        return [(number(z, c, (y + i) % rows, x), number(z, c, y, x)) for z, c, y, x in every]

    def right_of(z, c, y, x):
        if which(z, x) == 0:
            return number(z, c, y, 1 - x)
        return number(z + 1, c, y, x) if z + 1 < planes else None

    right = [
        (number(z, c, y, x), number(0, c, y, 0) if right_of(z, c, y, x) is None else right_of(z, c, y, x))
        for z, c, y, x in every
    ]
    end = which(planes - 1, 1)
    edge_route = [
        (number(planes - 1, c, y, 1 - end), number(planes - 1, c, y, end)) for y in range(rows) for c in (1 - end,)
    ]

    def move(block, route):
        return lax.ppermute(block, AXES, route)

    def move_or_keep(block, route):
        keeps = [a for a, b in route if a == b]
        moved = move(block, [(a, b) for a, b in route if a != b])
        return jnp.where(functools.reduce(jnp.logical_or, [me == a for a in keeps], me < 0), block, moved)

    col, tile = lax.axis_index("col"), lax.axis_index("tile")
    z, c, y, x = col // 2, col % 2, tile // 2, tile % 2
    s = (x + z) % 2
    site_number = 2 * z + s
    me = col * tiles + tile
    own_column = c == s

    share, legs, width = boundary.shape[1:]
    size = width // tiles

    small = jnp.concatenate(
        [
            sketch_phys[0].reshape(legs * legs, width).astype(F32),
            jnp.pad(
                jnp.concatenate([row_tensors[0].reshape(-1).astype(F32), closing[0]]),
                (0, width - legs**4 - legs),
            )[None],
        ]
    )
    small = jnp.where(own_column, small, move(small, core))
    row_tensor = small[-1, : legs**4].reshape(legs, legs, legs, legs)
    weights = small[-1, legs**4 : legs**4 + legs]
    phys_map = jnp.einsum(
        "lurd,ldk->kur",
        row_tensor,
        small[:-1].reshape(legs, legs, width),
        precision=lax.Precision.HIGHEST,
    ).reshape(width, legs * legs)
    step = size // (legs * legs)
    mix = jnp.einsum("lurd,ab->dlaurb", row_tensor, jnp.eye(step, dtype=F32))
    mix = mix.reshape(legs * legs * step, legs * legs * step).astype(BF16)

    ahead = jnp.arange(rows, dtype=jnp.int32)
    near = 2 * ((y + ahead) % rows) + (x + c + ahead) % 2
    far = 2 * ((y + ahead) % rows) + (x + c + ahead + 1) % 2
    spots = jnp.concatenate([near, far]).astype(jnp.int32)

    def after(value, *earlier):
        return lax.optimization_barrier((value, *earlier))[0]

    bonds = [move_or_keep(sketch_bond[0], fetch(i)) for i in range(rows)]
    site = after(boundary[0].transpose(1, 0, 2), *bonds)
    edge = after(edge_factor, bonds[-1]).transpose(2, 1, 0).reshape(width, legs * share)
    phys_map, mix, edge = lax.optimization_barrier((phys_map, mix, edge))
    near_site = move(site, [(a, b) for a, b in fetch(0) if a != b])
    keep = functools.reduce(jnp.logical_or, [me == a for a, b in fetch(0) if a == b], me < 0)
    choices = [(near_site, site)]
    flags = [keep.astype(jnp.int32)]
    second = [[(a, b) for a, b in fetch(i) if (b // tiles) % 2 == 1] for i in range(1, rows)]
    direct = [move(site, route) for route in second]
    for i in range(1, rows):
        route = [(a, b) for a, b in fetch(i) if (b // tiles) % 2 == 0]
        choices.append((move(after(site, near_site, *direct, edge, phys_map, mix), route), direct[i - 1]))
        flags.append(c.astype(jnp.int32))
    arrived = choices[-1][0]
    bonds += [move(b, core) for b in bonds]

    range_rows, panels, sites = [], [], []
    for choice, flag in zip(choices, flags):
        if panels:
            choice = (after(choice[0], panels[-1][0]), choice[1])
        rows_t, chosen_site, own = sketch(jnp.concatenate([spots, flag[None]]), phys_map, bonds, choice)
        range_rows.append(rows_t)
        sites.append(chosen_site)
        panels.append(own)
    others = [[move(p, core) for p in own] for own in panels[:-1]]
    first = move(panels[-1][0], core)
    others.append([first] + [move(after(p, first), core) for p in panels[-1][1:]])
    all_panels = [[own[turn] for own in panels + others] for turn in range(tiles)]
    sites += [move(after(b, *others[-1]), core) for b in sites]

    edges = [edge, move(after(edge, arrived), edge_route)]
    sender = jnp.where(site_number == columns - 1, jnp.where(c == x, 1, 2), 0).astype(jnp.int32)[None]

    lows, highs, rests, comes, turns, swaps = [], [], [], [], [], []

    def turn_round(come):
        return [move(come, turned(i)) for i in range(1, rows)]

    def swap(blocks):
        return [move(b, core) for b in blocks]

    for turn in range(tiles):
        parts = all_panels[turn]
        if turn >= 2:
            comes[turn - 2] = after(comes[turn - 2], highs[turn - 1][0])
            past = [comes[turn - 2]] + (turns[turn - 3] + swaps[turn - 3][:1] if turn >= 3 else sites[rows:])
            parts = [after(parts[0], *past)] + parts[1:]
            if turn >= 3:
                turns[turn - 3] = [after(b, highs[turn - 1][0]) for b in turns[turn - 3]]
                swaps[turn - 3] += swap(turns[turn - 3])
            turns.append(turn_round(comes[turn - 2]))
            swaps.append(swap(comes[turn - 2 : turn - 1]))
        out = basis_columns(turn, sender, edges, parts, lows, highs, rests, range_rows)
        highs.append(out[:rows])
        comes.append(move(out[rows], right))
        if turn < tiles - 1:
            rests.append(out[rows + 1])
            lows.append(out[rows + 2])

    def picked(q):
        out = list(highs[0])
        for turn in range(1, tiles):
            out = [jnp.where(q == turn, new, old) for new, old in zip(highs[turn], out)]
        return out

    basis_b = [move(b, core) for b in picked(far[0])]
    basis_a = picked(near[0])
    basis_a[0] = after(basis_a[0], *[b for blocks in swaps for b in blocks], *turns[-1])
    comes[-2] = after(comes[-2], highs[-1][0])
    turns.append(turn_round(comes[-2]))
    swaps.append(swap(comes[-2:-1]))
    absorbed = absorb(mix, basis_a + basis_b, sites, 0, tiles // 2)
    mix, comes[-1], absorbed, turns[-2], turns[-1], swaps[-1] = lax.optimization_barrier(
        (mix, comes[-1], absorbed, turns[-2], turns[-1], swaps[-1])
    )
    come = comes[-1]
    swaps[-2] += swap(turns[-2])
    swaps[-1] += swap(turns[-1])
    turns.append(turn_round(come))
    swaps.append(swap([come]))
    absorbed = absorb(mix, basis_a + basis_b, sites, tiles // 2, tiles - tiles // 2, absorbed)
    absorbed, last, _ = lax.optimization_barrier((absorbed, turns[-1], swaps))
    swaps[-1] += swap(last)
    lefts = [[come] + blocks + others_ for come, blocks, others_ in zip(comes, turns, swaps)]

    source = jnp.where(s == 1, 1 - x, x)
    near_left = 2 * ((y + ahead) % rows) + (source + c) % 2
    far_left = 2 * ((y + ahead) % rows) + (source + c + 1) % 2
    left_spots = jnp.concatenate([near_left, far_left]).astype(jnp.int32)
    near_own = 2 * ((y + ahead) % rows) + (x + c) % 2
    far_own = 2 * ((y + ahead) % rows) + (x + c + 1) % 2
    own_spots = jnp.concatenate([near_own, far_own]).astype(jnp.int32)

    new_early, transfer_early = close(left_spots, weights, absorbed, lefts[:-1], 0)
    transfer_early = [transfer_early] + [move(transfer_early, turned(i)) for i in range(1, rows)]
    home_moves = [(a, b) for a, b in home if a != b]
    new_late, transfer_late = close(
        left_spots, weights, after(absorbed, transfer_early[0]), lefts[-1:], tiles - 1, new_early
    )
    transfer_early += swap([after(t, transfer_late) for t in transfer_early])
    transfer_late = [transfer_late] + [move(transfer_late, turned(i)) for i in range(1, rows)]
    transfer_late += swap(transfer_late)
    transfers = [list(pair) for pair in zip(transfer_early, transfer_late)]

    starts = [d for d in every if right_of(*d) is not None]
    kept = left_edge[None]
    for turn in range(columns):
        env = kept
        if turn:
            route = [(number(*d), right_of(*d)) for d in starts if 2 * d[0] + which(d[0], d[3]) == turn - 1]
            env = move(kept, route)
        info = jnp.concatenate([own_spots, (site_number == turn).astype(jnp.int32)[None]])
        riders = []
        if turn == 2:
            moved_home = move(after(new_late, kept), home_moves)
        if turn == columns - 1:
            stays = functools.reduce(jnp.logical_or, [me == a for a, b in home if a == b], me < 0)
            new_site = settle(
                (1 - stays.astype(jnp.int32))[None], [(new_late, moved_home)]
            )
            riders = [new_site]
        kept = relay(info, env, kept, transfers, *riders)
    env = jnp.where(own_column, kept, move(kept, cross))
    env = lax.dynamic_slice_in_dim(env, tile * share, share, axis=1)
    return new_site[None], env


def solution(mesh):
    in_specs = (
        P("col", "tile", None, None),
        P("col", None, None, None, None),
        P("col", "tile", None),
        P("col", None, None, None),
        P("tile", None, None),
        P("col", None),
        P(),
    )
    out_specs = (P("col", "tile", None, None), P("col", "tile"))
    columns, tiles = mesh.shape["col"], mesh.shape["tile"]

    def local(*args):
        share, legs, width = args[0].shape[1:]
        even = columns % 2 == 0 and tiles % 2 == 0
        if even and share % (2 * LANES) == 0 and share == width // tiles and legs**4 + legs <= width:
            return paired(columns, tiles, *args)
        return plain(*args)

    return jax.shard_map(local, mesh=mesh, in_specs=in_specs, out_specs=out_specs, check_vma=False)
```
